256 devices in a mesh: band: 8 (over x, core), col: 32 (over y, z).
Axes of the slice: x: 4, y: 4, z: 8, core: 2. Of those that a mesh axis runs over, the one named last changes fastest.
Arguments:
- grid_fourier: bfloat16 [2560, 64, 512], P(('band', 'col')), may hold values from -6 to 6
- legendre: bfloat16 [64, 2560, 1280], P('col', 'band'), may hold values from -0.125 to 0.125
- band_legendre: bfloat16 [8, 64, 1280, 1280], P('band', 'col'), may hold values from -0.15625 to 0.15625
- filters: float32 [8, 1280], P('band'), may hold values from 0.5 to 1.5
- vertical: float32 [8, 8, 8], P('band'), may hold values from -2 to 2
- spread: float32 [8, 1280, 256], P('band', 'col'), may hold values from 0.3 to 3
- lat_counts: int32 [8], P('band'), may hold values from 160 to 1280, as said below
- wavenumbers: int32 [64], replicated, may hold values from 0 to 1279, as said below
Outputs:
- grid_out: bfloat16 [2560, 64, 512], P(('band', 'col'))
The draws below stay inside these ranges and needn't reach their ends.
Inputs may be any that keep to these rules, and one draw needn't show every extreme that they name: Distinct zonal wavenumbers, one a slot; 0 and 1279 are always among them. `lat_counts`: latitudes of a band's reduced grid at or beyond its count lie outside that grid; some band has 1280 and some band has 160.
All inputs are finite; a program needn't handle non-finite values.
Results may differ from the reference program's by a relative error of at most 0.03.
Values may be sent and summed in bfloat16 or wider, within the bound.
No kernel may reach another device: no remote copies, remote signals or barrier semaphores. Data moves between devices by JAX's collectives and lax.ppermute only.
A program may use at most 128 MiB of HBM per device.

```python
import math
import jax
import jax.numpy as jnp
from jax import lax

NLAT = 2560
NN = 1280
LB = 1280
LEV = 8
NLON = 256
M = 64
BANDS = 8
COMP = 512
N_BAND = 8


def draw_lat_counts(key, part):
    key = jax.random.fold_in(key, 5)
    subkeys = jax.random.split(key, 3)
    lowest = max(LB // 8, 1)
    counts = jax.random.randint(subkeys[0], (BANDS,), lowest, LB + 1)
    top_band = jax.random.randint(subkeys[1], (), 0, BANDS)
    offset = jax.random.randint(subkeys[2], (), 1, BANDS)
    low_band = (top_band + offset) % BANDS
    positions = jnp.arange(BANDS)
    counts = jnp.where(positions == top_band, LB, counts)
    counts = jnp.where(positions == low_band, lowest, counts)
    return counts.astype(jnp.int32)


def draw_wavenumbers(key, part):
    key = jax.random.fold_in(key, 9)
    subkeys = jax.random.split(key, 2)
    interior = jax.random.permutation(subkeys[0], NN - 2)[:M - 2] + 1
    values = jnp.concatenate([jnp.array([0, NN - 1], dtype=jnp.int32), interior.astype(jnp.int32)])
    shuffle = jax.random.permutation(subkeys[1], M)
    return values[shuffle].astype(jnp.int32)


def steps_of(key, extent, pieces, least, high):
    factor_of = 1.0
    for position, blocks in pieces:
        draws = jax.random.uniform(jax.random.fold_in(jax.random.fold_in(key, 6), position), (blocks,), jnp.float32, least / len(pieces), high / len(pieces))
        factor_of = factor_of * jnp.repeat(jnp.exp(draws), extent[position] // blocks).reshape((-1,) + (1,) * (len(extent) - 1 - position))
    return factor_of


def bell_draw(key, extent, deviation, most, cuts=(), held_as=jnp.bfloat16):
    level = steps_of(key, extent, cuts, -0.22, 0.18) if cuts else 1.0
    result = jax.random.normal(key, extent, jnp.float32) * deviation * level
    return jnp.minimum(jnp.maximum(result, -most), most).astype(held_as)


def setup_inputs(seed: int = 0) -> dict:
    key_of = jax.random.split(jax.random.key(seed), 9)
    return {
        "grid_fourier": bell_draw(key_of[0], (NLAT, M, COMP), 1.0, 6.0, ((0, 256),)),
        "legendre": bell_draw(key_of[1], (M, NLAT, NN), NLAT ** -0.5, 0.125, ((0, 32), (1, 8))),
        "band_legendre": bell_draw(key_of[2], (BANDS, M, LB, NN), NN ** -0.5, 0.15625, ((0, 8), (1, 32))),
        "filters": jnp.clip(0.5 + 1.0 * jax.random.uniform(key_of[3], (BANDS, NN), jnp.float32) ** steps_of(key_of[3], (BANDS, NN), ((0, 8),), -0.2, 0.2), 0.5, 1.5),
        "vertical": bell_draw(key_of[4], (BANDS, LEV, LEV), LEV ** -0.5, 2.0, ((0, 8),), jnp.float32),
        "spread": jnp.clip(jnp.exp(math.log(3.0) - 2.3025851 * jax.random.uniform(key_of[5], (BANDS, LB, NLON), jnp.float32) ** steps_of(key_of[5], (BANDS, LB, NLON), ((0, 8), (1, 32)), -0.2, 0.2)), 0.3, 3.0),
        "lat_counts": draw_lat_counts(jax.random.fold_in(key_of[8], 71), 0),
        "wavenumbers": draw_wavenumbers(jax.random.fold_in(key_of[8], 71), 0),
    }


def make_table(wavenumbers, longitudes):
    scaling = 1.0 / math.sqrt(wavenumbers.shape[0])
    k_index = jnp.arange(longitudes, dtype=jnp.int32)
    phases = 97 * k_index[:, None] * wavenumbers[None, :].astype(jnp.int32) % 7919
    angles = phases.astype(jnp.float32) * (2.0 * math.pi / 7919.0)
    cosine = (jnp.cos(angles) * scaling).astype(jnp.bfloat16)
    sine_part = (-jnp.sin(angles) * scaling).astype(jnp.bfloat16)
    return jnp.concatenate([cosine, sine_part], axis=1)

def grid_section(heights, wave_table, vertical, weights):
    wave_count, lat_rows, channels = heights.shape
    levels = vertical.shape[0]
    half_width = channels // 2
    longitudes = wave_table.shape[0]
    stacked = heights.reshape(wave_count, lat_rows, 2, half_width).transpose(2, 0, 1, 3).reshape(2 * wave_count, lat_rows * half_width)
    points = jnp.dot(wave_table, stacked, preferred_element_type=jnp.float32)
    points = points.reshape(longitudes, lat_rows, half_width // levels, levels)
    mixing = jnp.einsum('klvj,ij->klvi', points, vertical, precision=lax.Precision.HIGHEST)
    shaped = (mixing * weights[:, :, None, None]).astype(jnp.bfloat16).reshape(longitudes, lat_rows * half_width)
    returned = lax.dot_general(wave_table, shaped, (((0,), (0,)), ((), ())), preferred_element_type=jnp.float32)
    returned = returned.reshape(2, wave_count, lat_rows, half_width).transpose(1, 2, 0, 3).reshape(wave_count, lat_rows, channels)
    return returned.astype(jnp.bfloat16)

def reference(grid_fourier, legendre, band_legendre, filters, vertical, spread, lat_counts, wavenumbers):
    lat_total, wave_count, channels = grid_fourier.shape
    block_rows = lat_total // N_BAND

    def forward_slot(slot_index):
        leg_blocks = legendre[slot_index].reshape(N_BAND, block_rows, NN).astype(jnp.float32)
        data_blocks = grid_fourier[:, slot_index, :].reshape(N_BAND, block_rows, channels).astype(jnp.float32)
        partial_sums = jnp.einsum('bln,blc->bnc', leg_blocks, data_blocks).astype(jnp.bfloat16)
        return lax.optimization_barrier(jnp.sum(partial_sums.astype(jnp.float32), axis=0))
    spectrum = lax.map(forward_slot, jnp.arange(wave_count, dtype=jnp.int32))
    triangle = (jnp.arange(NN, dtype=jnp.int32)[None, :] >= wavenumbers[:, None].astype(jnp.int32)).astype(jnp.float32)
    wave_table = make_table(wavenumbers, NLON)

    def one_band(band_index):
        shape_band = filters[band_index][None, :] * triangle
        filtered = (spectrum * shape_band[:, :, None]).astype(jnp.bfloat16)
        band_leg = band_legendre[band_index]

        def raise_slot(slot_index):
            return jnp.dot(band_leg[slot_index], filtered[slot_index], preferred_element_type=jnp.float32)
        heights = lax.map(raise_slot, jnp.arange(wave_count, dtype=jnp.int32)).astype(jnp.bfloat16)
        live_rows = (jnp.arange(LB, dtype=jnp.int32) < lat_counts[band_index]).astype(jnp.float32)
        weights = (spread[band_index] * live_rows[:, None]).T
        returned = grid_section(heights, wave_table, vertical[band_index], weights)

        def lower_slot(slot_index):
            return lax.dot_general(band_leg[slot_index], returned[slot_index], (((0,), (0,)), ((), ())), preferred_element_type=jnp.float32)
        contrib = lax.map(lower_slot, jnp.arange(wave_count, dtype=jnp.int32)) * shape_band[:, :, None]
        return contrib.astype(jnp.bfloat16)
    all_contribs = lax.map(one_band, jnp.arange(N_BAND, dtype=jnp.int32))
    summed = lax.optimization_barrier(jnp.sum(all_contribs.astype(jnp.float32), axis=0)).astype(jnp.bfloat16)

    def back_slot(slot_index):
        return jnp.dot(legendre[slot_index], summed[slot_index], preferred_element_type=jnp.float32).astype(jnp.bfloat16)
    grid_out = lax.map(back_slot, jnp.arange(wave_count, dtype=jnp.int32))
    return jnp.transpose(grid_out, (1, 0, 2))
```

```python
import math
import jax
import jax.numpy as jnp
from jax import lax
from jax.experimental import pallas as pl
from jax.experimental.pallas import tpu as pltpu
from jax.sharding import PartitionSpec as P

F32, BF16 = jnp.float32, jnp.bfloat16
VMEM_LIMIT = 48 << 20
COLS = 32
ROWS = 8
HALF = 256


def params():
    return pltpu.CompilerParams(vmem_limit_bytes=VMEM_LIMIT)


def make_table(wavenumbers, longitudes):
    scaling = 1.0 / math.sqrt(wavenumbers.shape[0])
    k_index = jnp.arange(longitudes, dtype=jnp.int32)
    phases = 97 * k_index[:, None] * wavenumbers[None, :] % 7919
    angles = phases.astype(F32) * (2.0 * math.pi / 7919.0)
    cosine = (jnp.cos(angles) * scaling).astype(BF16)
    sine_part = (-jnp.sin(angles) * scaling).astype(BF16)
    return jnp.concatenate([cosine, sine_part], axis=1)


def band_sum(p):
    bi = lax.axis_index("band")
    core, xi = bi % 2, bi // 2
    swap = [(b, b ^ 1) for b in range(8)]
    shift = lambda k: [(b, ((b // 2 + k) % 4) * 2 + b % 2) for b in range(8)]
    rows, n = p.shape[1:]
    mine = lax.dynamic_index_in_dim(p, core, 0, False)
    other = lax.dynamic_index_in_dim(p, 1 - core, 0, False)
    got = lax.ppermute(other, "band", swap)
    s = (mine.astype(F32) + got.astype(F32)).reshape(4, rows // 4, n)
    sb = s.astype(BF16)
    acc = lax.dynamic_index_in_dim(s, xi, 0, False)
    for k in (1, 3, 2):
        snd = lax.dynamic_index_in_dim(sb, (xi + k) % 4, 0, False)
        acc = acc + lax.ppermute(snd, "band", shift(k)).astype(F32)
    r = acc.astype(BF16)
    full = jnp.zeros((4, rows // 4, n), BF16)
    full = lax.dynamic_update_index_in_dim(full, r, xi, 0)
    for k in (1, 3, 2):
        full = lax.dynamic_update_index_in_dim(full, lax.ppermute(r, "band", shift(k)), (xi - k) % 4, 0)
    full = full.reshape(rows, n)
    oth = lax.ppermute(full, "band", swap)
    lo = jnp.where(core == 0, full, oth)
    hi = jnp.where(core == 0, oth, full)
    return jnp.stack([lo, hi])


def raise_kernel(spec_ref, shape_ref, leg_ref, out_ref, filt_ref):
    @pl.when(pl.program_id(0) == 0)
    def _():
        for m in range(2):
            filt_ref[m] = (spec_ref[m].astype(F32) * shape_ref[m]).T.astype(BF16)

    rows = []
    for m in range(2):
        out = jnp.dot(leg_ref[m], filt_ref[m], preferred_element_type=F32)
        rows.append(out.reshape(COLS, ROWS, HALF))
    out_ref[...] = jnp.concatenate(rows, axis=1).astype(BF16)


def raise_heights(spec, shape_band, leg, blocks):
    slots, _, nn = leg.shape
    step = COLS * ROWS
    return pl.pallas_call(
        raise_kernel,
        grid=(blocks,),
        in_specs=[
            pl.BlockSpec((slots, HALF, nn), lambda t: (0, 0, 0)),
            pl.BlockSpec((slots, 1, nn), lambda t: (0, 0, 0)),
            pl.BlockSpec((slots, step, nn), lambda t: (0, t, 0)),
        ],
        out_specs=pl.BlockSpec((COLS, slots * ROWS, HALF), lambda t: (0, t, 0)),
        out_shape=jax.ShapeDtypeStruct((COLS, slots * ROWS * blocks, HALF), BF16),
        scratch_shapes=[pltpu.VMEM((slots, nn, HALF), BF16)],
        cost_estimate=pl.CostEstimate(
            flops=2 * slots * blocks * step * nn * HALF, bytes_accessed=2 * slots * blocks * step * nn, transcendentals=0
        ),
        compiler_params=params(),
    )(spec, shape_band, leg)


def lower_kernel(ret_ref, shape_ref, leg_ref, out_ref, turned_ref):
    blocks = ret_ref.shape[1] // (2 * ROWS)
    step = COLS * ROWS

    @pl.when(pl.program_id(0) == 0)
    def _():
        for t in range(blocks):
            both = ret_ref[:, t * 2 * ROWS : (t + 1) * 2 * ROWS, :].astype(F32)
            for m in range(2):
                part = both[:, m * ROWS : (m + 1) * ROWS, :].reshape(step, HALF)
                turned_ref[m, :, t * step : (t + 1) * step] = part.T.astype(BF16)

    for m in range(2):
        out = jnp.dot(turned_ref[m], leg_ref[m], preferred_element_type=F32)
        out_ref[m] = (out * shape_ref[m]).astype(BF16)


def lower_heights(ret, shape_band, leg, blocks):
    slots, _, nn = leg.shape
    lats = COLS * ROWS * blocks
    wide = 256
    return pl.pallas_call(
        lower_kernel,
        grid=(nn // wide,),
        in_specs=[
            pl.BlockSpec((COLS, slots * ROWS * blocks, HALF), lambda t: (0, 0, 0)),
            pl.BlockSpec((slots, 1, wide), lambda t: (0, 0, t)),
            pl.BlockSpec((slots, lats, wide), lambda t: (0, 0, t)),
        ],
        out_specs=pl.BlockSpec((slots, HALF, wide), lambda t: (0, 0, t)),
        out_shape=jax.ShapeDtypeStruct((slots, HALF, nn), BF16),
        scratch_shapes=[pltpu.VMEM((slots, HALF, lats), BF16)],
        cost_estimate=pl.CostEstimate(
            flops=2 * slots * lats * nn * HALF, bytes_accessed=2 * slots * lats * nn, transcendentals=0
        ),
        compiler_params=params(),
    )(ret, shape_band, leg)


def grid_kernel(x_ref, mix_ref, wave_ref, turned_ref, weight_ref, out_ref, in_ref, back_ref):
    tall = x_ref.shape[1]
    blocks = tall // (2 * ROWS)
    group = 4
    lanes = HALF // 2

    def mix(g, carry):
        rows = x_ref[pl.ds(g * group, group)].astype(F32).reshape(group * tall, HALF).astype(BF16)
        got = jnp.dot(rows, mix_ref[0], preferred_element_type=F32)
        got += jnp.dot(rows, mix_ref[1], preferred_element_type=F32)
        for r in range(2):
            in_ref[r, pl.ds(pl.multiple_of(g * (group * tall), 8), group * tall), :] = got[:, r * lanes : (r + 1) * lanes]
        return carry

    lax.fori_loop(0, COLS // group, mix, 0)

    def block(t, carry):
        scale = weight_ref[t]
        for pair in range(ROWS // 2):
            sides = []
            for half in range(2):
                parts = []
                for r in range(2):
                    for m in range(2):
                        start = t * (2 * ROWS) + (m * ROWS + 2 * pair + half)
                        parts.append(in_ref[r, pl.ds(start, COLS, stride=tall), :])
                sides.append(jnp.concatenate(parts, axis=0))
            waves = jnp.concatenate(sides, axis=1).astype(BF16)
            points = jnp.dot(wave_ref[...], waves, preferred_element_type=F32)
            shaped = []
            for half in range(2):
                l = 2 * pair + half
                shaped.append((points[:, half * lanes : (half + 1) * lanes] * scale[:, l : l + 1]).astype(BF16))
            returned = jnp.dot(turned_ref[...], jnp.concatenate(shaped, axis=1), preferred_element_type=F32)
            for half in range(2):
                for r in range(2):
                    for m in range(2):
                        start = t * (2 * ROWS) + (m * ROWS + 2 * pair + half)
                        row = (r * 2 + m) * COLS
                        back_ref[r, pl.ds(start, COLS, stride=tall), :] = returned[
                            row : row + COLS, half * lanes : (half + 1) * lanes
                        ]
        return carry

    lax.fori_loop(0, blocks, block, 0)

    def leave(g, carry):
        rows = jnp.concatenate(
            [back_ref[r, pl.ds(pl.multiple_of(g * (group * tall), 8), group * tall), :] for r in range(2)], axis=1
        )
        out_ref[pl.ds(g * group, group)] = rows.reshape(group, tall, HALF).astype(BF16)
        return carry

    lax.fori_loop(0, COLS // group, leave, 0)


def grid_section(x, mix, wave, turned, weight):
    cols, tall, c = x.shape
    blocks = tall // (2 * ROWS)
    longs = wave.shape[0]
    return pl.pallas_call(
        grid_kernel,
        grid=(1,),
        in_specs=[
            pl.BlockSpec(x.shape, lambda t: (0, 0, 0)),
            pl.BlockSpec(mix.shape, lambda t: (0, 0, 0)),
            pl.BlockSpec(wave.shape, lambda t: (0, 0)),
            pl.BlockSpec(turned.shape, lambda t: (0, 0)),
            pl.BlockSpec((blocks,) + weight.shape[1:], lambda t: (0, 0, 0)),
        ],
        out_specs=pl.BlockSpec(x.shape, lambda t: (0, 0, 0)),
        out_shape=jax.ShapeDtypeStruct(x.shape, BF16),
        scratch_shapes=[pltpu.VMEM((2, cols * tall, c // 2), F32), pltpu.VMEM((2, cols * tall, c // 2), F32)],
        cost_estimate=pl.CostEstimate(
            flops=4 * longs * 128 * blocks * ROWS * (c // 2), bytes_accessed=4 * cols * tall * c, transcendentals=0
        ),
        compiler_params=params(),
    )(x, mix, wave, turned, weight)


def spread_blocks(spread, ci):
    per = spread.shape[0] // ROWS
    own = spread.reshape(per, ROWS, spread.shape[1])
    got = [lax.ppermute(own[i], "col", [(e, (per * e + i) % COLS) for e in range(COLS)]) for i in range(per)]
    return jnp.stack([
        lax.dynamic_index_in_dim(jnp.stack(got), (ci + COLS * q) % per, 0, False) for q in range(per)
    ])


def per_device(grid_fourier, legendre, band_legendre, filters, vertical, spread, lat_counts, wavenumbers):
    ci = lax.axis_index("col")
    slots, lats, nn = legendre.shape
    per = spread.shape[1] // ROWS
    rows = grid_fourier.shape[0]
    own = lax.dynamic_slice_in_dim(wavenumbers, ci * slots, slots)
    tri = (jnp.arange(nn, dtype=jnp.int32)[None, :] >= own[:, None]).astype(F32)
    shape_band = (filters[0][None, :] * tri)[:, None, :]
    wave = make_table(wavenumbers.reshape(COLS, slots).T.reshape(-1), spread.shape[2])
    turned = wave.T
    spreads = spread_blocks(spread[0], ci)
    index = (jnp.arange(per)[:, None] * COLS + ci) * ROWS + jnp.arange(ROWS)[None, :]
    live = (index < lat_counts[0]).astype(F32)
    weight = (spreads * live[:, :, None]).transpose(0, 2, 1)
    mix = jnp.kron(jnp.eye(HALF // vertical.shape[1], dtype=F32), vertical[0].T)
    coarse = lax.reduce_precision(mix, 8, 7)
    mix = jnp.stack([coarse.astype(BF16), (mix - coarse).astype(BF16)])
    bl = band_legendre[0]
    tie = lax.optimization_barrier
    a2a = lambda x: lax.all_to_all(x, "col", 0, 0, tiled=True)

    snd = grid_fourier.reshape(rows, COLS, slots, 2, 2, 128).transpose(1, 4, 2, 0, 3, 5)
    got = a2a(snd.reshape(COLS, 2 * slots * rows, HALF)).reshape(COLS, 2, slots, rows, HALF)
    parts = []
    for h in range(2):
        d = got[:, h].transpose(1, 0, 2, 3).reshape(slots, COLS * rows, HALF)
        parts.append(jnp.einsum("mln,mlc->mcn", legendre, d, preferred_element_type=F32).astype(BF16))

    def middle(blocks):
        def run(spec):
            x = a2a(raise_heights(spec, shape_band, bl, blocks))
            x = a2a(grid_section(x, mix, wave, turned, weight))
            return lower_heights(x, shape_band, bl, blocks)

        return run

    branches = [middle(b + 1) for b in range(per)]
    choice = (lat_counts[0] + (COLS * ROWS - 1)) // (COLS * ROWS) - 1
    spec_a = band_sum(parts[0])
    spec_b = lax.psum(parts[1], "band")
    con_a = lax.switch(choice, branches, spec_a)
    con_a, spec_b = tie((con_a, spec_b))
    sum_a = lax.psum(con_a, "band")
    con_b = lax.switch(choice, branches, spec_b)
    con_b, sum_a = tie((con_b, sum_a))
    sum_b = band_sum(con_b)
    outs = []
    for s in (sum_a, sum_b):
        r = jnp.einsum("mln,mcn->mlc", legendre, s, preferred_element_type=F32).astype(BF16)
        outs.append(r.reshape(slots, COLS, rows, HALF).transpose(1, 0, 2, 3))
    snd = jnp.stack(outs, axis=1).reshape(COLS, 2 * slots * rows, HALF)
    got = a2a(snd).reshape(COLS, 2, slots, rows, 2, 128)
    return got.transpose(3, 0, 2, 4, 1, 5).reshape(rows, COLS * slots, 2 * HALF)


def solution(mesh):
    in_specs = (
        P(("band", "col"), None, None),
        P("col", "band", None),
        P("band", "col", None, None),
        P("band", None),
        P("band", None, None),
        P("band", "col", None),
        P("band"),
        P(),
    )
    out_specs = P(("band", "col"), None, None)
    return jax.shard_map(per_device, mesh=mesh, in_specs=in_specs, out_specs=out_specs, check_vma=False)
```

```python
import math
import jax
import jax.numpy as jnp
from jax import lax
from jax.experimental import pallas as pl
from jax.experimental.pallas import tpu as pltpu
from jax.sharding import PartitionSpec as P

F32, BF16 = jnp.float32, jnp.bfloat16
VMEM_LIMIT = 48 << 20
COLS = 32
ROWS = 8
HALF = 256


def params():
    return pltpu.CompilerParams(vmem_limit_bytes=VMEM_LIMIT)


def make_table(wavenumbers, longitudes):
    scaling = 1.0 / math.sqrt(wavenumbers.shape[0])
    k_index = jnp.arange(longitudes, dtype=jnp.int32)
    phases = 97 * k_index[:, None] * wavenumbers[None, :] % 7919
    angles = phases.astype(F32) * (2.0 * math.pi / 7919.0)
    cosine = (jnp.cos(angles) * scaling).astype(BF16)
    sine_part = (-jnp.sin(angles) * scaling).astype(BF16)
    return jnp.concatenate([cosine, sine_part], axis=1)


def band_sum(p):
    bi = lax.axis_index("band")
    core, xi = bi % 2, bi // 2
    swap = [(b, b ^ 1) for b in range(8)]
    shift = lambda k: [(b, ((b // 2 + k) % 4) * 2 + b % 2) for b in range(8)]
    rows, n = p.shape[1:]
    mine = lax.dynamic_index_in_dim(p, core, 0, False)
    other = lax.dynamic_index_in_dim(p, 1 - core, 0, False)
    got = lax.ppermute(other, "band", swap)
    s = (mine.astype(F32) + got.astype(F32)).reshape(4, rows // 4, n)
    sb = s.astype(BF16)
    acc = lax.dynamic_index_in_dim(s, xi, 0, False)
    for k in (1, 3, 2):
        snd = lax.dynamic_index_in_dim(sb, (xi + k) % 4, 0, False)
        acc = acc + lax.ppermute(snd, "band", shift(k)).astype(F32)
    r = acc.astype(BF16)
    full = jnp.zeros((4, rows // 4, n), BF16)
    full = lax.dynamic_update_index_in_dim(full, r, xi, 0)
    for k in (1, 3, 2):
        full = lax.dynamic_update_index_in_dim(full, lax.ppermute(r, "band", shift(k)), (xi - k) % 4, 0)
    full = full.reshape(rows, n)
    oth = lax.ppermute(full, "band", swap)
    return full, oth


def in_order(core, own, oth):
    return jnp.stack([jnp.where(core == 0, own, oth), jnp.where(core == 0, oth, own)])


def raise_kernel(core_ref, own_ref, oth_ref, shape_ref, leg_ref, out_ref, filt_ref):
    @pl.when(pl.program_id(0) == 0)
    def _():
        for m in range(2):
            spec = jnp.where(core_ref[0] == m, own_ref[...], oth_ref[...]).astype(F32)
            filt_ref[m] = (spec * shape_ref[m]).T.astype(BF16)

    rows = []
    for m in range(2):
        out = jnp.dot(leg_ref[m], filt_ref[m], preferred_element_type=F32)
        rows.append(out.reshape(COLS, ROWS, HALF))
    out_ref[...] = jnp.concatenate(rows, axis=1).astype(BF16)


def raise_heights(core, own, oth, shape_band, leg):
    slots, lats, nn = leg.shape
    step = COLS * ROWS
    blocks = lats // step
    return pl.pallas_call(
        raise_kernel,
        grid_spec=pltpu.PrefetchScalarGridSpec(
            num_scalar_prefetch=1,
            grid=(blocks,),
            in_specs=[
                pl.BlockSpec((HALF, nn), lambda t, c: (0, 0)),
                pl.BlockSpec((HALF, nn), lambda t, c: (0, 0)),
                pl.BlockSpec((slots, 1, nn), lambda t, c: (0, 0, 0)),
                pl.BlockSpec((slots, step, nn), lambda t, c: (0, t, 0)),
            ],
            out_specs=pl.BlockSpec((COLS, slots * ROWS, HALF), lambda t, c: (0, t, 0)),
            scratch_shapes=[pltpu.VMEM((slots, nn, HALF), BF16)],
        ),
        out_shape=jax.ShapeDtypeStruct((COLS, slots * ROWS * blocks, HALF), BF16),
        cost_estimate=pl.CostEstimate(
            flops=2 * slots * lats * nn * HALF, bytes_accessed=2 * slots * lats * nn, transcendentals=0
        ),
        compiler_params=params(),
    )(core, own, oth, shape_band, leg)


def lower_kernel(ret_ref, shape_ref, leg_ref, out_ref, turned_ref):
    blocks = ret_ref.shape[1] // (2 * ROWS)
    step = COLS * ROWS

    @pl.when(pl.program_id(0) == 0)
    def _():
        for t in range(blocks):
            both = ret_ref[:, t * 2 * ROWS : (t + 1) * 2 * ROWS, :].astype(F32)
            for m in range(2):
                part = both[:, m * ROWS : (m + 1) * ROWS, :].reshape(step, HALF)
                turned_ref[m, :, t * step : (t + 1) * step] = part.T.astype(BF16)

    for m in range(2):
        out = jnp.dot(turned_ref[m], leg_ref[m], preferred_element_type=F32)
        out_ref[m] = (out * shape_ref[m]).astype(BF16)


def lower_heights(ret, shape_band, leg, blocks):
    slots, _, nn = leg.shape
    lats = COLS * ROWS * blocks
    wide = 640
    return pl.pallas_call(
        lower_kernel,
        grid=(nn // wide,),
        in_specs=[
            pl.BlockSpec((COLS, slots * ROWS * blocks, HALF), lambda t: (0, 0, 0)),
            pl.BlockSpec((slots, 1, wide), lambda t: (0, 0, t)),
            pl.BlockSpec((slots, lats, wide), lambda t: (0, 0, t)),
        ],
        out_specs=pl.BlockSpec((slots, HALF, wide), lambda t: (0, 0, t)),
        out_shape=jax.ShapeDtypeStruct((slots, HALF, nn), BF16),
        scratch_shapes=[pltpu.VMEM((slots, HALF, lats), BF16)],
        cost_estimate=pl.CostEstimate(
            flops=2 * slots * lats * nn * HALF, bytes_accessed=2 * slots * lats * nn, transcendentals=0
        ),
        compiler_params=params(),
    )(ret, shape_band, leg)


def grid_kernel(x_ref, mix_ref, wave_ref, turned_ref, weight_ref, out_ref, in_ref, back_ref):
    tall = x_ref.shape[1]
    over = out_ref.shape[1] - tall
    blocks = tall // (2 * ROWS)
    group = 4
    lanes = HALF // 2

    def mix(g, carry):
        rows = x_ref[pl.ds(g * group, group)].astype(F32).reshape(group * tall, HALF).astype(BF16)
        got = jnp.dot(rows, mix_ref[0], preferred_element_type=F32)
        got += jnp.dot(rows, mix_ref[1], preferred_element_type=F32)
        for r in range(2):
            in_ref[r, pl.ds(pl.multiple_of(g * (group * tall), 8), group * tall), :] = got[:, r * lanes : (r + 1) * lanes]
        return carry

    lax.fori_loop(0, COLS // group, mix, 0)

    def block(t, carry):
        scale = weight_ref[t]
        for pair in range(ROWS // 2):
            sides = []
            for half in range(2):
                parts = []
                for r in range(2):
                    for m in range(2):
                        start = t * (2 * ROWS) + (m * ROWS + 2 * pair + half)
                        parts.append(in_ref[r, pl.ds(start, COLS, stride=tall), :])
                sides.append(jnp.concatenate(parts, axis=0))
            waves = jnp.concatenate(sides, axis=1).astype(BF16)
            points = jnp.dot(wave_ref[...], waves, preferred_element_type=F32)
            shaped = []
            for half in range(2):
                l = 2 * pair + half
                shaped.append((points[:, half * lanes : (half + 1) * lanes] * scale[:, l : l + 1]).astype(BF16))
            returned = jnp.dot(turned_ref[...], jnp.concatenate(shaped, axis=1), preferred_element_type=F32)
            for half in range(2):
                for r in range(2):
                    for m in range(2):
                        start = t * (2 * ROWS) + (m * ROWS + 2 * pair + half)
                        row = (r * 2 + m) * COLS
                        back_ref[r, pl.ds(start, COLS, stride=tall), :] = returned[
                            row : row + COLS, half * lanes : (half + 1) * lanes
                        ]
        return carry

    lax.fori_loop(0, blocks, block, 0)

    def leave(g, carry):
        rows = jnp.concatenate(
            [back_ref[r, pl.ds(pl.multiple_of(g * (group * tall), 8), group * tall), :] for r in range(2)], axis=1
        )
        out_ref[pl.ds(g * group, group), :tall] = rows.reshape(group, tall, HALF).astype(BF16)
        if over:
            out_ref[pl.ds(g * group, group), tall:] = jnp.zeros((group, over, HALF), BF16)
        return carry

    lax.fori_loop(0, COLS // group, leave, 0)


def grid_section(x, mix, wave, turned, weight, blocks, out):
    cols, _, c = x.shape
    tall = 2 * ROWS * blocks
    longs = wave.shape[0]
    return pl.pallas_call(
        grid_kernel,
        grid=(1,),
        in_specs=[
            pl.BlockSpec((cols, tall, c), lambda t: (0, 0, 0)),
            pl.BlockSpec(mix.shape, lambda t: (0, 0, 0)),
            pl.BlockSpec(wave.shape, lambda t: (0, 0)),
            pl.BlockSpec(turned.shape, lambda t: (0, 0)),
            pl.BlockSpec((blocks,) + weight.shape[1:], lambda t: (0, 0, 0)),
        ],
        out_specs=pl.BlockSpec((cols, out, c), lambda t: (0, 0, 0)),
        out_shape=jax.ShapeDtypeStruct((cols, out, c), BF16),
        scratch_shapes=[pltpu.VMEM((2, cols * tall, c // 2), F32), pltpu.VMEM((2, cols * tall, c // 2), F32)],
        cost_estimate=pl.CostEstimate(
            flops=4 * longs * 128 * blocks * ROWS * (c // 2), bytes_accessed=4 * cols * tall * c, transcendentals=0
        ),
        compiler_params=params(),
    )(x, mix, wave, turned, weight)


def send_spread(spread, ci):
    own = spread.reshape(-1, ROWS, spread.shape[1]).astype(BF16)
    per = own.shape[0]
    ring = jnp.zeros((COLS + per,) + own.shape[1:], BF16)
    ring = lax.dynamic_update_slice_in_dim(ring, own, per * ci % COLS, 0)
    return jnp.concatenate([ring[:per] + ring[COLS:], ring[per:COLS]])


def take_spread(got, ci, per):
    return jnp.stack([lax.dynamic_index_in_dim(got, (COLS * q + ci) // per, 0, False) for q in range(per)])


def per_device(grid_fourier, legendre, band_legendre, filters, vertical, spread, lat_counts, wavenumbers):
    ci = lax.axis_index("col")
    slots, lats, nn = legendre.shape
    per = spread.shape[1] // ROWS
    rows = grid_fourier.shape[0]
    own = lax.dynamic_slice_in_dim(wavenumbers, ci * slots, slots)
    tri = (jnp.arange(nn, dtype=jnp.int32)[None, :] >= own[:, None]).astype(F32)
    shape_band = (filters[0][None, :] * tri)[:, None, :]
    bl = band_legendre[0]
    tie = lax.optimization_barrier
    a2a = lambda x: lax.all_to_all(x, "col", 0, 0, tiled=True)

    pack = 2 * rows
    per_half = ROWS // 2
    spread_rows = send_spread(spread[0], ci)
    snd = grid_fourier.reshape(rows, COLS, slots, 2, 2, 128).transpose(4, 1, 2, 0, 3, 5)
    snd = snd.reshape(2, COLS, pack, HALF)
    snd_a = jnp.concatenate([snd[0], spread_rows[:, :per_half]], axis=1)
    snd_b = jnp.concatenate([snd[1], spread_rows[:, per_half:]], axis=1)
    core = (lax.axis_index("band") % 2).astype(jnp.int32)
    core1 = core.reshape(1)
    some = wavenumbers[0] >= 0

    def together(f, *args):
        shapes = jax.eval_shape(f, *args)
        return lax.cond(some, f, lambda *_: jax.tree.map(lambda x: jnp.zeros(x.shape, x.dtype), shapes), *args)

    def analyse(got):
        d = got[:, :pack].reshape(COLS, slots, rows, HALF).transpose(1, 0, 2, 3).reshape(slots, COLS * rows, HALF)
        part = jnp.einsum("mln,mlc->mcn", legendre, d, preferred_element_type=F32).astype(BF16)
        return raise_heights(core1, *band_sum(part), shape_band, bl)

    def first(got):
        levels = vertical.shape[1]
        lane = jnp.arange(HALF, dtype=jnp.int32)
        pick = (lane[:, None] % levels == jnp.arange(levels, dtype=jnp.int32)[None, :]).astype(F32)
        same = (lane[:, None] // levels == lane[None, :] // levels).astype(F32)
        exact = lambda x, y: jnp.dot(x, y, precision=lax.Precision.HIGHEST)
        mix = exact(pick, exact(vertical[0].T, pick.T)) * same
        coarse = lax.reduce_precision(mix, 8, 7)
        mix = jnp.stack([coarse.astype(BF16), (mix - coarse).astype(BF16)])
        wave = make_table(wavenumbers.reshape(COLS, slots).T.reshape(-1), spread.shape[2])
        return analyse(got), mix, wave, wave.T

    def second(got_a, got_b):
        index = (jnp.arange(per)[:, None] * COLS + ci) * ROWS + jnp.arange(ROWS)[None, :]
        live = (index < lat_counts[0]).astype(F32)
        got = jnp.concatenate([got_a[:, pack:], got_b[:, pack:]], axis=1)
        weight = (take_spread(got, ci, per).astype(F32) * live[:, :, None]).transpose(0, 2, 1)
        return analyse(got_b), weight

    def last(back):
        own, oth = band_sum(lower_heights(back, shape_band, bl, per))
        r = jnp.einsum("mln,mcn->mlc", legendre, in_order(core, own, oth), preferred_element_type=F32)
        return r.astype(BF16).reshape(slots, COLS, rows, HALF).transpose(1, 0, 2, 3).reshape(COLS, pack, HALF)

    def middle(blocks):
        tall = 2 * ROWS * blocks

        def run(far_a, high_b, mix, wave, turned, weight):
            section = lambda x, out: grid_section(x, mix, wave, turned, weight, blocks, out)
            far_b = a2a(high_b[:, :tall])
            far_b, ret_a = tie((far_b, section(far_a, tall)))
            back_a = a2a(ret_a)
            ret_b = section(far_b, high_b.shape[1])
            back_a = jnp.pad(back_a, ((0, 0), (0, high_b.shape[1] - tall), (0, 0)))
            return back_a, ret_b

        return run

    branches = [middle(per - b) for b in range(per)]
    choice = per - (lat_counts[0] + (COLS * ROWS - 1)) // (COLS * ROWS)

    got_a = a2a(snd_a)
    got_a, snd_b = tie((got_a, snd_b))
    got_b = a2a(snd_b)
    high_a, mix, wave, turned = together(first, got_a)
    high_a, got_b = tie((high_a, got_b))
    far_a = a2a(high_a)
    high_b, weight = together(second, got_a, got_b)
    far_a, high_b = tie((far_a, high_b))
    back_a, ret_b = lax.switch(choice, branches, far_a, high_b, mix, wave, turned, weight)
    back_b = a2a(ret_b)
    out_a = together(last, back_a)
    back_b, out_a = tie((back_b, out_a))
    end_a = a2a(out_a)
    out_b = together(last, back_b)
    end_a, out_b = tie((end_a, out_b))
    got = jnp.stack([end_a, a2a(out_b)], axis=1).reshape(COLS, 2, slots, rows, 2, 128)
    return got.transpose(3, 0, 2, 4, 1, 5).reshape(rows, COLS * slots, 2 * HALF)


def solution(mesh):
    in_specs = (
        P(("band", "col"), None, None),
        P("col", "band", None),
        P("band", "col", None, None),
        P("band", None),
        P("band", None, None),
        P("band", "col", None),
        P("band"),
        P(),
    )
    out_specs = P(("band", "col"), None, None)
    return jax.shard_map(per_device, mesh=mesh, in_specs=in_specs, out_specs=out_specs, check_vma=False)
```

```python
import math
import jax
import jax.numpy as jnp
from jax import lax
from jax.experimental import pallas as pl
from jax.experimental.pallas import tpu as pltpu
from jax.sharding import PartitionSpec as P

F32, BF16 = jnp.float32, jnp.bfloat16
VMEM_LIMIT = 48 << 20
COLS = 32
ROWS = 8
HALF = 256


def params():
    return pltpu.CompilerParams(vmem_limit_bytes=VMEM_LIMIT)


def make_table(wavenumbers, longitudes):
    scaling = 1.0 / math.sqrt(wavenumbers.shape[0])
    k_index = jnp.arange(longitudes, dtype=jnp.int32)
    phases = 97 * k_index[:, None] * wavenumbers[None, :] % 7919
    angles = phases.astype(F32) * (2.0 * math.pi / 7919.0)
    cosine = (jnp.cos(angles) * scaling).astype(BF16)
    sine_part = (-jnp.sin(angles) * scaling).astype(BF16)
    return jnp.concatenate([cosine, sine_part], axis=1)


def band_sum(mine, other):
    bi = lax.axis_index("band")
    xi = (bi // 2).astype(jnp.int32)
    swap = [(b, b ^ 1) for b in range(8)]
    shift = lambda k: [(b, ((b // 2 + k) % 4) * 2 + b % 2) for b in range(8)]
    rows, n = mine.shape
    got = lax.ppermute(other, "band", swap)
    s = (mine.astype(F32) + got.astype(F32)).reshape(4, rows // 4, n)
    sb = s.astype(BF16)
    acc = lax.dynamic_index_in_dim(s, xi, 0, False)
    for k in (1, 3, 2):
        snd = lax.dynamic_index_in_dim(sb, (xi + k) % 4, 0, False)
        acc = acc + lax.ppermute(snd, "band", shift(k)).astype(F32)
    r = acc.astype(BF16)
    quarters = [r] + [lax.ppermute(r, "band", shift(k)) for k in (1, 2, 3)]
    full = jnp.concatenate([lax.select_n((xi - j) % 4, *quarters) for j in range(4)])
    return full, lax.ppermute(full, "band", swap)


def by_core(core, p):
    return lax.dynamic_index_in_dim(p, core, 0, False), lax.dynamic_index_in_dim(p, 1 - core, 0, False)


def in_order(core, own, oth):
    return jnp.stack([jnp.where(core == 0, own, oth), jnp.where(core == 0, oth, own)])


def raise_kernel(core_ref, own_ref, oth_ref, shape_ref, leg_ref, out_ref, filt_ref):
    @pl.when(pl.program_id(0) == 0)
    def _():
        wide = 256
        chunks = own_ref.shape[1] // wide

        def turn(i, carry):
            m = i // chunks
            span = pl.ds(pl.multiple_of(i % chunks * wide, wide), wide)
            spec = jnp.where(core_ref[0] == m, own_ref[:, span], oth_ref[:, span]).astype(F32)
            filt_ref[m, span, :] = (spec * shape_ref[m, :, span]).T.astype(BF16)
            return carry

        lax.fori_loop(0, 2 * chunks, turn, 0)

    rows = []
    for m in range(2):
        out = jnp.dot(leg_ref[m], filt_ref[m], preferred_element_type=F32)
        rows.append(out.reshape(COLS, ROWS, HALF))
    out_ref[...] = jnp.concatenate(rows, axis=1).astype(BF16)


def raise_heights(core, own, oth, shape_band, leg, blocks):
    slots, _, nn = leg.shape
    step = COLS * ROWS
    lats = blocks * step
    return pl.pallas_call(
        raise_kernel,
        grid_spec=pltpu.PrefetchScalarGridSpec(
            num_scalar_prefetch=1,
            grid=(blocks,),
            in_specs=[
                pl.BlockSpec((HALF, nn), lambda t, c: (0, 0)),
                pl.BlockSpec((HALF, nn), lambda t, c: (0, 0)),
                pl.BlockSpec((slots, 1, nn), lambda t, c: (0, 0, 0)),
                pl.BlockSpec((slots, step, nn), lambda t, c: (0, t, 0)),
            ],
            out_specs=pl.BlockSpec((COLS, slots * ROWS, HALF), lambda t, c: (0, t, 0)),
            scratch_shapes=[pltpu.VMEM((slots, nn, HALF), BF16)],
        ),
        out_shape=jax.ShapeDtypeStruct((COLS, slots * ROWS * blocks, HALF), BF16),
        cost_estimate=pl.CostEstimate(
            flops=2 * slots * lats * nn * HALF, bytes_accessed=2 * slots * lats * nn, transcendentals=0
        ),
        compiler_params=params(),
    )(core, own, oth, shape_band, leg)


def lower_kernel(core_ref, ret_ref, shape_own, shape_oth, leg_own, leg_oth, own_ref, oth_ref, turned_ref):
    blocks = ret_ref.shape[1] // (2 * ROWS)
    step = COLS * ROWS

    @pl.when(pl.program_id(0) == 0)
    def _():
        def turn(t, carry):
            both = ret_ref[:, pl.ds(pl.multiple_of(t * 2 * ROWS, 2 * ROWS), 2 * ROWS), :].astype(F32)
            for m in range(2):
                part = both[:, m * ROWS : (m + 1) * ROWS, :].reshape(step, HALF)
                turned_ref[m, :, pl.ds(pl.multiple_of(t * step, step), step)] = part.T.astype(BF16)
            return carry

        lax.fori_loop(0, blocks, turn, 0)

    core = core_ref[0]
    own = jnp.dot(turned_ref[core], leg_own[0], preferred_element_type=F32)
    own_ref[...] = (own * shape_own[0]).astype(BF16)
    oth = jnp.dot(turned_ref[1 - core], leg_oth[0], preferred_element_type=F32)
    oth_ref[...] = (oth * shape_oth[0]).astype(BF16)


def lower_heights(core, ret, shape_band, leg, blocks):
    slots, _, nn = leg.shape
    lats = COLS * ROWS * blocks
    wide = 256
    return pl.pallas_call(
        lower_kernel,
        grid_spec=pltpu.PrefetchScalarGridSpec(
            num_scalar_prefetch=1,
            grid=(nn // wide,),
            in_specs=[
                pl.BlockSpec((COLS, slots * ROWS * blocks, HALF), lambda t, c: (0, 0, 0)),
                pl.BlockSpec((1, 1, wide), lambda t, c: (c[0], 0, t)),
                pl.BlockSpec((1, 1, wide), lambda t, c: (1 - c[0], 0, t)),
                pl.BlockSpec((1, lats, wide), lambda t, c: (c[0], 0, t)),
                pl.BlockSpec((1, lats, wide), lambda t, c: (1 - c[0], 0, t)),
            ],
            out_specs=[pl.BlockSpec((HALF, wide), lambda t, c: (0, t)), pl.BlockSpec((HALF, wide), lambda t, c: (0, t))],
            scratch_shapes=[pltpu.VMEM((slots, HALF, lats), BF16)],
        ),
        out_shape=[jax.ShapeDtypeStruct((HALF, nn), BF16), jax.ShapeDtypeStruct((HALF, nn), BF16)],
        cost_estimate=pl.CostEstimate(
            flops=2 * slots * lats * nn * HALF, bytes_accessed=2 * slots * lats * nn, transcendentals=0
        ),
        compiler_params=params(),
    )(core, ret, shape_band, shape_band, leg, leg)


def grid_kernel(x_ref, mix_ref, wave_ref, turned_ref, weight_ref, out_ref, in_ref, back_ref):
    tall = x_ref.shape[1]
    over = out_ref.shape[1] - tall
    blocks = tall // (2 * ROWS)
    group = 4
    lanes = HALF // 2

    def mix(g, carry):
        rows = x_ref[pl.ds(g * group, group)].astype(F32).reshape(group * tall, HALF).astype(BF16)
        got = jnp.dot(rows, mix_ref[0], preferred_element_type=F32)
        got += jnp.dot(rows, mix_ref[1], preferred_element_type=F32)
        for r in range(2):
            in_ref[r, pl.ds(pl.multiple_of(g * (group * tall), 8), group * tall), :] = got[:, r * lanes : (r + 1) * lanes]
        return carry

    lax.fori_loop(0, COLS // group, mix, 0)

    def block(t, carry):
        scale = weight_ref[t]
        for pair in range(ROWS // 2):
            sides = []
            for half in range(2):
                parts = []
                for r in range(2):
                    for m in range(2):
                        start = t * (2 * ROWS) + (m * ROWS + 2 * pair + half)
                        parts.append(in_ref[r, pl.ds(start, COLS, stride=tall), :])
                sides.append(jnp.concatenate(parts, axis=0))
            waves = jnp.concatenate(sides, axis=1).astype(BF16)
            points = jnp.dot(wave_ref[...], waves, preferred_element_type=F32)
            shaped = []
            for half in range(2):
                l = 2 * pair + half
                shaped.append((points[:, half * lanes : (half + 1) * lanes] * scale[:, l : l + 1]).astype(BF16))
            returned = jnp.dot(turned_ref[...], jnp.concatenate(shaped, axis=1), preferred_element_type=F32)
            for half in range(2):
                for r in range(2):
                    for m in range(2):
                        start = t * (2 * ROWS) + (m * ROWS + 2 * pair + half)
                        row = (r * 2 + m) * COLS
                        back_ref[r, pl.ds(start, COLS, stride=tall), :] = returned[
                            row : row + COLS, half * lanes : (half + 1) * lanes
                        ]
        return carry

    lax.fori_loop(0, blocks, block, 0)

    def leave(g, carry):
        rows = jnp.concatenate(
            [back_ref[r, pl.ds(pl.multiple_of(g * (group * tall), 8), group * tall), :] for r in range(2)], axis=1
        )
        out_ref[pl.ds(g * group, group), :tall] = rows.reshape(group, tall, HALF).astype(BF16)
        if over:
            out_ref[pl.ds(g * group, group), tall:] = jnp.zeros((group, over, HALF), BF16)
        return carry

    lax.fori_loop(0, COLS // group, leave, 0)


def grid_section(x, mix, wave, turned, weight, blocks, out):
    cols, _, c = x.shape
    tall = 2 * ROWS * blocks
    longs = wave.shape[0]
    return pl.pallas_call(
        grid_kernel,
        grid=(1,),
        in_specs=[
            pl.BlockSpec((cols, tall, c), lambda t: (0, 0, 0)),
            pl.BlockSpec(mix.shape, lambda t: (0, 0, 0)),
            pl.BlockSpec(wave.shape, lambda t: (0, 0)),
            pl.BlockSpec(turned.shape, lambda t: (0, 0)),
            pl.BlockSpec((blocks,) + weight.shape[1:], lambda t: (0, 0, 0)),
        ],
        out_specs=pl.BlockSpec((cols, out, c), lambda t: (0, 0, 0)),
        out_shape=jax.ShapeDtypeStruct((cols, out, c), BF16),
        scratch_shapes=[pltpu.VMEM((2, cols * tall, c // 2), F32), pltpu.VMEM((2, cols * tall, c // 2), F32)],
        cost_estimate=pl.CostEstimate(
            flops=4 * longs * 128 * blocks * ROWS * (c // 2), bytes_accessed=4 * cols * tall * c, transcendentals=0
        ),
        compiler_params=params(),
    )(x, mix, wave, turned, weight)


def send_spread(spread, ci):
    own = spread.reshape(-1, ROWS, spread.shape[1]).astype(BF16)
    per = own.shape[0]
    ring = jnp.zeros((COLS + per,) + own.shape[1:], BF16)
    ring = lax.dynamic_update_slice_in_dim(ring, own, per * ci % COLS, 0)
    return jnp.concatenate([ring[:per] + ring[COLS:], ring[per:COLS]])


def take_spread(got, ci, per):
    return jnp.stack([lax.dynamic_index_in_dim(got, (COLS * q + ci) // per, 0, False) for q in range(per)])


def per_device(grid_fourier, legendre, band_legendre, filters, vertical, spread, lat_counts, wavenumbers):
    ci = lax.axis_index("col")
    slots, lats, nn = legendre.shape
    per = spread.shape[1] // ROWS
    rows = grid_fourier.shape[0]
    own = lax.dynamic_slice_in_dim(wavenumbers, ci * slots, slots)
    tri = (jnp.arange(nn, dtype=jnp.int32)[None, :] >= own[:, None]).astype(F32)
    shape_band = (filters[0][None, :] * tri)[:, None, :]
    wave = make_table(wavenumbers.reshape(COLS, slots).T.reshape(-1), spread.shape[2])
    turned = wave.T
    index = (jnp.arange(per)[:, None] * COLS + ci) * ROWS + jnp.arange(ROWS)[None, :]
    live = (index < lat_counts[0]).astype(F32)
    levels = vertical.shape[1]
    lane = jnp.arange(HALF, dtype=jnp.int32)
    pick = (lane[:, None] % levels == jnp.arange(levels, dtype=jnp.int32)[None, :]).astype(F32)
    same = (lane[:, None] // levels == lane[None, :] // levels).astype(F32)
    exact = lambda x, y: jnp.dot(x, y, precision=lax.Precision.HIGHEST)
    mix = exact(pick, exact(vertical[0].T, pick.T)) * same
    coarse = lax.reduce_precision(mix, 8, 7)
    mix = jnp.stack([coarse.astype(BF16), (mix - coarse).astype(BF16)])
    bl = band_legendre[0]
    tie = lax.optimization_barrier
    a2a = lambda x: lax.all_to_all(x, "col", 0, 0, tiled=True)

    snd = grid_fourier.reshape(rows, COLS, slots, 2, 2, 128).transpose(1, 4, 2, 0, 3, 5)
    snd = jnp.concatenate([snd.reshape(COLS, 2 * slots * rows, HALF), send_spread(spread[0], ci)], axis=1)
    got = a2a(snd)
    weight = (take_spread(got[:, 2 * slots * rows :], ci, per).astype(F32) * live[:, :, None]).transpose(0, 2, 1)
    got = got[:, : 2 * slots * rows].reshape(COLS, 2, slots, rows, HALF)
    parts = []
    for h in range(2):
        d = got[:, h].transpose(1, 0, 2, 3).reshape(slots, COLS * rows, HALF)
        parts.append(jnp.einsum("mln,mlc->mcn", legendre, d, preferred_element_type=F32).astype(BF16))

    core = (lax.axis_index("band") % 2).astype(jnp.int32)
    core1 = core.reshape(1)

    def middle(blocks):
        raised = lambda own, oth: raise_heights(core1, own, oth, shape_band, bl, blocks)
        section = lambda x: grid_section(x, mix, wave, turned, weight, blocks, x.shape[1])
        lowered = lambda x: lower_heights(core1, x, shape_band, bl, blocks)

        def run(own_a, oth_a, own_b, oth_b):
            far_a = a2a(raised(own_a, oth_a))
            far_a, high_b = tie((far_a, raised(own_b, oth_b)))
            far_b = a2a(high_b)
            far_b, ret_a = tie((far_b, section(far_a)))
            back_a = a2a(ret_a)
            back_a, ret_b = tie((back_a, section(far_b)))
            back_b = a2a(ret_b)
            return (*lowered(back_a), *lowered(back_b))

        return run

    branches = [middle(b + 1) for b in range(per)]
    choice = (lat_counts[0] + (COLS * ROWS - 1)) // (COLS * ROWS) - 1
    specs = (*band_sum(*by_core(core, parts[0])), *band_sum(*by_core(core, parts[1])))
    cons = lax.switch(choice, branches, *specs)
    sum_a, sum_b = in_order(core, *band_sum(*cons[:2])), in_order(core, *band_sum(*cons[2:]))
    outs = []
    for s in (sum_a, sum_b):
        r = jnp.einsum("mln,mcn->mlc", legendre, s, preferred_element_type=F32).astype(BF16)
        outs.append(r.reshape(slots, COLS, rows, HALF).transpose(1, 0, 2, 3))
    snd = jnp.stack(outs, axis=1).reshape(COLS, 2 * slots * rows, HALF)
    got = a2a(snd).reshape(COLS, 2, slots, rows, 2, 128)
    return got.transpose(3, 0, 2, 4, 1, 5).reshape(rows, COLS * slots, 2 * HALF)


def solution(mesh):
    in_specs = (
        P(("band", "col"), None, None),
        P("col", "band", None),
        P("band", "col", None, None),
        P("band", None),
        P("band", None, None),
        P("band", "col", None),
        P("band"),
        P(),
    )
    out_specs = P(("band", "col"), None, None)
    return jax.shard_map(per_device, mesh=mesh, in_specs=in_specs, out_specs=out_specs, check_vma=False)
```

```python
import math
import jax
import jax.numpy as jnp
from jax import lax
from jax.experimental import pallas as pl
from jax.experimental.pallas import tpu as pltpu
from jax.sharding import PartitionSpec as P

F32, BF16 = jnp.float32, jnp.bfloat16
VMEM_LIMIT = 48 << 20
COLS = 32
ROWS = 8
HALF = 256


def params():
    return pltpu.CompilerParams(vmem_limit_bytes=VMEM_LIMIT)


def make_table(wavenumbers, longitudes):
    scaling = 1.0 / math.sqrt(wavenumbers.shape[0])
    k_index = jnp.arange(longitudes, dtype=jnp.int32)
    phases = 97 * k_index[:, None] * wavenumbers[None, :] % 7919
    angles = phases.astype(F32) * (2.0 * math.pi / 7919.0)
    cosine = (jnp.cos(angles) * scaling).astype(BF16)
    sine_part = (-jnp.sin(angles) * scaling).astype(BF16)
    return jnp.concatenate([cosine, sine_part], axis=1)


def band_sum(mine, other):
    bi = lax.axis_index("band")
    xi = (bi // 2).astype(jnp.int32)
    swap = [(b, b ^ 1) for b in range(8)]
    shift = lambda k: [(b, ((b // 2 + k) % 4) * 2 + b % 2) for b in range(8)]
    rows, n = mine.shape
    got = lax.ppermute(other, "band", swap)
    s = (mine.astype(F32) + got.astype(F32)).reshape(4, rows // 4, n)
    sb = s.astype(BF16)
    acc = lax.dynamic_index_in_dim(s, xi, 0, False)
    for k in (1, 3, 2):
        snd = lax.dynamic_index_in_dim(sb, (xi + k) % 4, 0, False)
        acc = acc + lax.ppermute(snd, "band", shift(k)).astype(F32)
    r = acc.astype(BF16)
    quarters = [r] + [lax.ppermute(r, "band", shift(k)) for k in (1, 2, 3)]
    full = jnp.concatenate([lax.select_n((xi - j) % 4, *quarters) for j in range(4)])
    return full, lax.ppermute(full, "band", swap)


def by_core(core, p):
    return lax.dynamic_index_in_dim(p, core, 0, False), lax.dynamic_index_in_dim(p, 1 - core, 0, False)


def in_order(core, own, oth):
    return jnp.stack([jnp.where(core == 0, own, oth), jnp.where(core == 0, oth, own)])


def raise_kernel(core_ref, own_ref, oth_ref, shape_ref, leg_ref, out_ref, filt_ref):
    @pl.when(pl.program_id(0) == 0)
    def _():
        wide = 256
        chunks = own_ref.shape[1] // wide

        def turn(i, carry):
            m = i // chunks
            span = pl.ds(pl.multiple_of(i % chunks * wide, wide), wide)
            spec = jnp.where(core_ref[0] == m, own_ref[:, span], oth_ref[:, span]).astype(F32)
            filt_ref[m, span, :] = (spec * shape_ref[m, :, span]).T.astype(BF16)
            return carry

        lax.fori_loop(0, 2 * chunks, turn, 0)

    rows = []
    for m in range(2):
        out = jnp.dot(leg_ref[m], filt_ref[m], preferred_element_type=F32)
        rows.append(out.reshape(COLS, ROWS, HALF))
    out_ref[...] = jnp.concatenate(rows, axis=1).astype(BF16)


def raise_heights(core, own, oth, shape_band, leg, blocks):
    slots, _, nn = leg.shape
    step = COLS * ROWS
    lats = blocks * step
    return pl.pallas_call(
        raise_kernel,
        grid_spec=pltpu.PrefetchScalarGridSpec(
            num_scalar_prefetch=1,
            grid=(blocks,),
            in_specs=[
                pl.BlockSpec((HALF, nn), lambda t, c: (0, 0)),
                pl.BlockSpec((HALF, nn), lambda t, c: (0, 0)),
                pl.BlockSpec((slots, 1, nn), lambda t, c: (0, 0, 0)),
                pl.BlockSpec((slots, step, nn), lambda t, c: (0, t, 0)),
            ],
            out_specs=pl.BlockSpec((COLS, slots * ROWS, HALF), lambda t, c: (0, t, 0)),
            scratch_shapes=[pltpu.VMEM((slots, nn, HALF), BF16)],
        ),
        out_shape=jax.ShapeDtypeStruct((COLS, slots * ROWS * blocks, HALF), BF16),
        cost_estimate=pl.CostEstimate(
            flops=2 * slots * lats * nn * HALF, bytes_accessed=2 * slots * lats * nn, transcendentals=0
        ),
        compiler_params=params(),
    )(core, own, oth, shape_band, leg)


def lower_kernel(core_ref, ret_ref, shape_own, shape_oth, leg_own, leg_oth, own_ref, oth_ref, turned_ref):
    blocks = ret_ref.shape[1] // (2 * ROWS)
    step = COLS * ROWS

    @pl.when(pl.program_id(0) == 0)
    def _():
        def turn(t, carry):
            both = ret_ref[:, pl.ds(pl.multiple_of(t * 2 * ROWS, 2 * ROWS), 2 * ROWS), :].astype(F32)
            for m in range(2):
                part = both[:, m * ROWS : (m + 1) * ROWS, :].reshape(step, HALF)
                turned_ref[m, :, pl.ds(pl.multiple_of(t * step, step), step)] = part.T.astype(BF16)
            return carry

        lax.fori_loop(0, blocks, turn, 0)

    core = core_ref[0]
    own = jnp.dot(turned_ref[core], leg_own[0], preferred_element_type=F32)
    own_ref[...] = (own * shape_own[0]).astype(BF16)
    oth = jnp.dot(turned_ref[1 - core], leg_oth[0], preferred_element_type=F32)
    oth_ref[...] = (oth * shape_oth[0]).astype(BF16)


def lower_heights(core, ret, shape_band, leg, blocks):
    slots, _, nn = leg.shape
    lats = COLS * ROWS * blocks
    wide = 256
    return pl.pallas_call(
        lower_kernel,
        grid_spec=pltpu.PrefetchScalarGridSpec(
            num_scalar_prefetch=1,
            grid=(nn // wide,),
            in_specs=[
                pl.BlockSpec((COLS, slots * ROWS * blocks, HALF), lambda t, c: (0, 0, 0)),
                pl.BlockSpec((1, 1, wide), lambda t, c: (c[0], 0, t)),
                pl.BlockSpec((1, 1, wide), lambda t, c: (1 - c[0], 0, t)),
                pl.BlockSpec((1, lats, wide), lambda t, c: (c[0], 0, t)),
                pl.BlockSpec((1, lats, wide), lambda t, c: (1 - c[0], 0, t)),
            ],
            out_specs=[pl.BlockSpec((HALF, wide), lambda t, c: (0, t)), pl.BlockSpec((HALF, wide), lambda t, c: (0, t))],
            scratch_shapes=[pltpu.VMEM((slots, HALF, lats), BF16)],
        ),
        out_shape=[jax.ShapeDtypeStruct((HALF, nn), BF16), jax.ShapeDtypeStruct((HALF, nn), BF16)],
        cost_estimate=pl.CostEstimate(
            flops=2 * slots * lats * nn * HALF, bytes_accessed=2 * slots * lats * nn, transcendentals=0
        ),
        compiler_params=params(),
    )(core, ret, shape_band, shape_band, leg, leg)


def grid_kernel(x_ref, mix_ref, wave_ref, turned_ref, weight_ref, out_ref, in_ref, back_ref):
    tall = x_ref.shape[1]
    over = out_ref.shape[1] - tall
    blocks = tall // (2 * ROWS)
    group = 4
    lanes = HALF // 2

    def mix(g, carry):
        rows = x_ref[pl.ds(g * group, group)].astype(F32).reshape(group * tall, HALF).astype(BF16)
        got = jnp.dot(rows, mix_ref[0], preferred_element_type=F32)
        got += jnp.dot(rows, mix_ref[1], preferred_element_type=F32)
        for r in range(2):
            in_ref[r, pl.ds(pl.multiple_of(g * (group * tall), 8), group * tall), :] = got[:, r * lanes : (r + 1) * lanes]
        return carry

    lax.fori_loop(0, COLS // group, mix, 0)

    def block(t, carry):
        scale = weight_ref[t]
        for pair in range(ROWS // 2):
            sides = []
            for half in range(2):
                parts = []
                for r in range(2):
                    for m in range(2):
                        start = t * (2 * ROWS) + (m * ROWS + 2 * pair + half)
                        parts.append(in_ref[r, pl.ds(start, COLS, stride=tall), :])
                sides.append(jnp.concatenate(parts, axis=0))
            waves = jnp.concatenate(sides, axis=1).astype(BF16)
            points = jnp.dot(wave_ref[...], waves, preferred_element_type=F32)
            shaped = []
            for half in range(2):
                l = 2 * pair + half
                shaped.append((points[:, half * lanes : (half + 1) * lanes] * scale[:, l : l + 1]).astype(BF16))
            returned = jnp.dot(turned_ref[...], jnp.concatenate(shaped, axis=1), preferred_element_type=F32)
            for half in range(2):
                for r in range(2):
                    for m in range(2):
                        start = t * (2 * ROWS) + (m * ROWS + 2 * pair + half)
                        row = (r * 2 + m) * COLS
                        back_ref[r, pl.ds(start, COLS, stride=tall), :] = returned[
                            row : row + COLS, half * lanes : (half + 1) * lanes
                        ]
        return carry

    lax.fori_loop(0, blocks, block, 0)

    def leave(g, carry):
        rows = jnp.concatenate(
            [back_ref[r, pl.ds(pl.multiple_of(g * (group * tall), 8), group * tall), :] for r in range(2)], axis=1
        )
        out_ref[pl.ds(g * group, group), :tall] = rows.reshape(group, tall, HALF).astype(BF16)
        if over:
            out_ref[pl.ds(g * group, group), tall:] = jnp.zeros((group, over, HALF), BF16)
        return carry

    lax.fori_loop(0, COLS // group, leave, 0)


def grid_section(x, mix, wave, turned, weight, blocks, out):
    cols, _, c = x.shape
    tall = 2 * ROWS * blocks
    longs = wave.shape[0]
    return pl.pallas_call(
        grid_kernel,
        grid=(1,),
        in_specs=[
            pl.BlockSpec((cols, tall, c), lambda t: (0, 0, 0)),
            pl.BlockSpec(mix.shape, lambda t: (0, 0, 0)),
            pl.BlockSpec(wave.shape, lambda t: (0, 0)),
            pl.BlockSpec(turned.shape, lambda t: (0, 0)),
            pl.BlockSpec((blocks,) + weight.shape[1:], lambda t: (0, 0, 0)),
        ],
        out_specs=pl.BlockSpec((cols, out, c), lambda t: (0, 0, 0)),
        out_shape=jax.ShapeDtypeStruct((cols, out, c), BF16),
        scratch_shapes=[pltpu.VMEM((2, cols * tall, c // 2), F32), pltpu.VMEM((2, cols * tall, c // 2), F32)],
        cost_estimate=pl.CostEstimate(
            flops=4 * longs * 128 * blocks * ROWS * (c // 2), bytes_accessed=4 * cols * tall * c, transcendentals=0
        ),
        compiler_params=params(),
    )(x, mix, wave, turned, weight)


def send_spread(spread, ci):
    own = spread.reshape(-1, ROWS, spread.shape[1]).astype(BF16)
    per = own.shape[0]
    ring = jnp.zeros((COLS + per,) + own.shape[1:], BF16)
    ring = lax.dynamic_update_slice_in_dim(ring, own, per * ci % COLS, 0)
    return jnp.concatenate([ring[:per] + ring[COLS:], ring[per:COLS]])


def take_spread(got, ci, per):
    return jnp.stack([lax.dynamic_index_in_dim(got, (COLS * q + ci) // per, 0, False) for q in range(per)])


def per_device(grid_fourier, legendre, band_legendre, filters, vertical, spread, lat_counts, wavenumbers):
    ci = lax.axis_index("col")
    slots, lats, nn = legendre.shape
    per = spread.shape[1] // ROWS
    rows = grid_fourier.shape[0]
    own = lax.dynamic_slice_in_dim(wavenumbers, ci * slots, slots)
    tri = (jnp.arange(nn, dtype=jnp.int32)[None, :] >= own[:, None]).astype(F32)
    shape_band = (filters[0][None, :] * tri)[:, None, :]
    wave = make_table(wavenumbers.reshape(COLS, slots).T.reshape(-1), spread.shape[2])
    turned = wave.T
    index = (jnp.arange(per)[:, None] * COLS + ci) * ROWS + jnp.arange(ROWS)[None, :]
    live = (index < lat_counts[0]).astype(F32)
    levels = vertical.shape[1]
    lane = jnp.arange(HALF, dtype=jnp.int32)
    pick = (lane[:, None] % levels == jnp.arange(levels, dtype=jnp.int32)[None, :]).astype(F32)
    same = (lane[:, None] // levels == lane[None, :] // levels).astype(F32)
    exact = lambda x, y: jnp.dot(x, y, precision=lax.Precision.HIGHEST)
    mix = exact(pick, exact(vertical[0].T, pick.T)) * same
    coarse = lax.reduce_precision(mix, 8, 7)
    mix = jnp.stack([coarse.astype(BF16), (mix - coarse).astype(BF16)])
    bl = band_legendre[0]
    tie = lax.optimization_barrier
    a2a = lambda x: lax.all_to_all(x, "col", 0, 0, tiled=True)

    snd = grid_fourier.reshape(rows, COLS, slots, 2, 2, 128).transpose(1, 4, 2, 0, 3, 5)
    snd = jnp.concatenate([snd.reshape(COLS, 2 * slots * rows, HALF), send_spread(spread[0], ci)], axis=1)
    got = a2a(snd)
    weight = (take_spread(got[:, 2 * slots * rows :], ci, per).astype(F32) * live[:, :, None]).transpose(0, 2, 1)
    got = got[:, : 2 * slots * rows].reshape(COLS, 2, slots, rows, HALF)
    parts = []
    for h in range(2):
        d = got[:, h].transpose(1, 0, 2, 3).reshape(slots, COLS * rows, HALF)
        parts.append(jnp.einsum("mln,mlc->mcn", legendre, d, preferred_element_type=F32).astype(BF16))

    core = (lax.axis_index("band") % 2).astype(jnp.int32)
    core1 = core.reshape(1)

    def middle(blocks):
        raised = lambda own, oth: raise_heights(core1, own, oth, shape_band, bl, blocks)
        section = lambda x: grid_section(x, mix, wave, turned, weight, blocks, x.shape[1])
        lowered = lambda x: lower_heights(core1, x, shape_band, bl, blocks)

        def run(own_a, oth_a, own_b, oth_b):
            far_a = a2a(raised(own_a, oth_a))
            far_a, high_b = tie((far_a, raised(own_b, oth_b)))
            far_b = a2a(high_b)
            far_b, ret_a = tie((far_b, section(far_a)))
            back_a = a2a(ret_a)
            back_a, ret_b = tie((back_a, section(far_b)))
            back_b = a2a(ret_b)
            return (*lowered(back_a), *lowered(back_b))

        return run

    branches = [middle(b) for b in range(2, per + 1)]
    choice = jnp.maximum((lat_counts[0] + (COLS * ROWS - 1)) // (COLS * ROWS) - 2, 0)
    specs = (*band_sum(*by_core(core, parts[0])), *band_sum(*by_core(core, parts[1])))
    cons = lax.switch(choice, branches, *specs)
    sum_a, sum_b = in_order(core, *band_sum(*cons[:2])), in_order(core, *band_sum(*cons[2:]))
    outs = []
    for s in (sum_a, sum_b):
        r = jnp.einsum("mln,mcn->mlc", legendre, s, preferred_element_type=F32).astype(BF16)
        outs.append(r.reshape(slots, COLS, rows, HALF).transpose(1, 0, 2, 3))
    snd = jnp.stack(outs, axis=1).reshape(COLS, 2 * slots * rows, HALF)
    got = a2a(snd).reshape(COLS, 2, slots, rows, 2, 128)
    return got.transpose(3, 0, 2, 4, 1, 5).reshape(rows, COLS * slots, 2 * HALF)


def solution(mesh):
    in_specs = (
        P(("band", "col"), None, None),
        P("col", "band", None),
        P("band", "col", None, None),
        P("band", None),
        P("band", None, None),
        P("band", "col", None),
        P("band"),
        P(),
    )
    out_specs = P(("band", "col"), None, None)
    return jax.shard_map(per_device, mesh=mesh, in_specs=in_specs, out_specs=out_specs, check_vma=False)
```
